256 devices in a mesh: group: 8 (over y, core), tile: 32 (over z, x).
Axes of the slice: x: 4, y: 4, z: 8, core: 2. Of those that a mesh axis runs over, the one named last changes fastest.
Arguments:
- embeddings: bfloat16 [8, 16384, 768], P('group', 'tile'), may hold values from -30 to 30
- cluster_ids: int32 [8, 16384], P('group', 'tile'), may hold values from 0 to 7, never falling along the last dimension, each value on 1 to 12288 neighbouring positions
Outputs:
- duplicate_score: float32 [8, 16384], P('group', 'tile')
The draws below stay inside these ranges and needn't reach their ends.
Inputs may be any that keep to these rules, and one draw needn't show every extreme that they name: `cluster_ids`: within each cluster group the cluster numbers never fall along the member order; each cluster has 1 to 12288 members, and some cluster has exactly that many.
All inputs are finite; a program needn't handle non-finite values.
Results may differ from the reference program's by a relative error of at most 0.0005.
Values may be sent and summed in bfloat16 or wider, within the bound.
A program may use at most 128 MiB of HBM per device.

```python
import math
import jax
import jax.numpy as jnp
import numpy as np
from jax import lax

D = 768
GROUP_ROWS = 16384
SHARE = 64
N_GROUP = 8
N_TILE = 32


def draw_embeddings(key, part):
    key = jax.random.fold_in(key, 11)
    noise_key, order_key = jax.random.split(key, 2)
    base = jax.random.normal(noise_key, (N_GROUP, GROUP_ROWS, D), jnp.float32)
    orders = jax.vmap(lambda single: jax.random.permutation(single, GROUP_ROWS))(jax.random.split(order_key, N_GROUP))
    partner = jnp.take_along_axis(base, orders[:, :, None], axis=1)
    mixed = base + partner
    source = mixed.reshape(N_GROUP, N_TILE, N_GROUP, SHARE, D).transpose(2, 1, 0, 3, 4).reshape(N_GROUP, GROUP_ROWS, D)
    return source.astype(jnp.bfloat16)


def profile(amount, total, reach, slope):
    portions = [(1 << 20) // math.isqrt(standing ** slope) + 1 for standing in range(2, amount + 1)]
    rest, given = total - reach - (amount - 1), [1] * (amount - 1)
    while rest > 0:
        movable = [i for i in range(amount - 1) if given[i] < reach]
        whole, remaining = sum([portions[i] for i in movable]), rest
        for i in movable:
            addition = min(reach - given[i], max(1, remaining * portions[i] // whole), rest)
            given[i] = given[i] + addition
            rest = rest - addition
    return np.array([reach] + given)


def ragged_sizes(key, count, total, limit, skew):
    if count == 2:
        one = jax.random.randint(key, (), max(1, total - limit), min(limit, total - 1) + 1)
        return jnp.stack([one, total - one])
    lengths = jnp.asarray(profile(count, total, limit, skew), jnp.int32)
    couples = (count - 1) // 2
    giver, receiver = lengths[1:1 + 2 * couples:2], lengths[2:2 + 2 * couples:2]
    slack = jnp.minimum(giver - 1, limit - receiver)
    shifted = jax.random.randint(jax.random.fold_in(key, 1), (couples,), 0, 1 << 20) % (slack + 1)
    lengths = lengths.at[1:1 + 2 * couples:2].set(giver - shifted).at[2:2 + 2 * couples:2].set(receiver + shifted)
    return lengths[jax.random.permutation(jax.random.fold_in(key, 2), count)]


def setup_inputs(seed: int = 0) -> dict:
    seeds = jax.random.split(jax.random.key(seed), 3)
    return {
        "embeddings": draw_embeddings(jax.random.fold_in(seeds[2], 71), 0),
        "cluster_ids": jax.vmap(lambda own: jnp.searchsorted(jnp.cumsum(ragged_sizes(own, N_TILE // 4, GROUP_ROWS, 3 * GROUP_ROWS // 4, 2)), jnp.arange(GROUP_ROWS), side="right"))(jax.random.split(seeds[1], N_GROUP)).reshape((N_GROUP, GROUP_ROWS)).astype(jnp.int32),
    }


def reference(embeddings, cluster_ids):
    values = embeddings.astype(jnp.float32)
    unit = (values / jnp.sqrt(lax.optimization_barrier(jnp.sum(values * values, axis=-1, keepdims=True)) + 1e-06)).astype(jnp.bfloat16)
    member = unit.reshape(N_GROUP, N_TILE, N_GROUP, SHARE, D).transpose(2, 1, 0, 3, 4).reshape(N_GROUP, GROUP_ROWS, D)
    block = math.gcd(GROUP_ROWS, 512)

    def one_group(operands):
        group_rows, group_ids = operands
        widened = group_rows.astype(jnp.float32)
        position = jnp.arange(GROUP_ROWS, dtype=jnp.int32)

        def one_block(first):
            part = lax.dynamic_slice_in_dim(widened, first, block, 0)
            part_ids = lax.dynamic_slice_in_dim(group_ids, first, block, 0)
            part_index = first + jnp.arange(block, dtype=jnp.int32)
            scores = jnp.dot(part, widened.T, precision=lax.Precision.HIGHEST)
            keep = (part_ids[:, None] == group_ids[None, :]) & (part_index[:, None] != position[None, :])
            return lax.optimization_barrier(jnp.max(jnp.where(keep, scores, -1.0), axis=1))
        firsts = jnp.arange(0, GROUP_ROWS, block, dtype=jnp.int32)
        return lax.map(one_block, firsts).reshape(GROUP_ROWS)
    nearest = lax.map(one_group, (member, cluster_ids))
    return nearest.reshape(N_GROUP, N_TILE, N_GROUP, SHARE).transpose(2, 1, 0, 3).reshape(N_GROUP, GROUP_ROWS)
```

```python
import functools

import jax
import jax.numpy as jnp
from jax import lax
from jax.experimental import pallas as pl
from jax.experimental.pallas import tpu as pltpu
from jax.sharding import PartitionSpec as P

MESH = pl.DeviceIdType.MESH
D = 768
ROWS = 512
PIECE = 64

COVER = ((0, 0), (0, 1), (0, -1), (1, -1), (-1, -1), (2, -1))
SIBLING = (0, 1, 3)
OFFSETS = (0, 1, -1, 2, -2, 3, -3, 4)
STEPS = ((0, 1), (1, 1), (2, 2), (4, 2), (6, 2))
SENT = ((1, 2), (3, 4), (5, 6), (7,), (), ())
FULL = ((0, 2), (0, 3), (0, 4), (0, 5), (2, 3), (1, 6), (2, 6), (4, 6), (5, 6), (4, 8), (5, 8))
HALF = ((1, 2, 0), (1, 3, 0), (1, 4, 0), (1, 5, 0), (2, 5, 1), (0, 6, 2), (3, 6, 2), (1, 7, 2), (3, 8, 2))


def pick(n, table):
    value = jnp.int32(table[0])
    for at in range(1, len(table)):
        value = jnp.where(n == at, jnp.int32(table[at]), value)
    return value


def kernel(
    x_ref, bound_ref, out_ref,
    unit, slots, idr, idc, rowacc, colacc, res, inb, near, obuf,
    z_send, z_recv, t_send, t_recv, r_send, r_recv, o_send, o_recv,
):
    group = lax.axis_index("group")
    tile = lax.axis_index("tile")
    y, c = group // 2, group % 2
    z, x = tile // 4, tile % 4
    flip = c == 1
    u = jnp.where(flip, y, x)
    v = jnp.where(flip, x, y)

    def chip(du, dv, other):
        nu, nv = (u + du + 4) % 4, (v + dv + 4) % 4
        nx = jnp.where(flip, nv, nu)
        ny = jnp.where(flip, nu, nv)
        nc = 1 - c if other else c
        return {"group": ny * 2 + nc, "tile": z * 4 + nx}

    def plane(dz):
        return {"group": group, "tile": ((z + dz + 8) % 8) * 4 + x}

    barrier = pltpu.get_barrier_semaphore()
    partners = [plane(o) for o in range(1, 8)]
    partners += [chip(a, b, False) for a, b in ((0, 1), (0, -1), (1, 0), (-1, 0), (1, -1), (-1, 1), (-1, -1), (1, 1), (2, -1), (2, 1))]
    partners += [chip(a, b, True) for a, b in ((0, 0), (1, 0), (0, -1), (-1, 1))]
    for partner in partners:
        pl.semaphore_signal(barrier, inc=1, device_id=partner, device_id_type=MESH)

    def normalize(p):
        k = (z - OFFSETS[p] + 8) % 8
        values = x_ref[0, pl.ds(pl.multiple_of(k * PIECE, PIECE), PIECE), :].astype(jnp.float32)
        total = jnp.sum(values * values, axis=1, keepdims=True) + 1e-06
        return (values * (1.0 / jnp.sqrt(total))).astype(jnp.bfloat16)

    slots[0, 0:PIECE, :] = normalize(0)
    for p in range(1, 8):
        unit[p] = normalize(p)

    pl.semaphore_wait(barrier, len(partners))

    def z_copy(p):
        return pltpu.make_async_remote_copy(
            src_ref=unit.at[p],
            dst_ref=slots.at[0, pl.ds(p * PIECE, PIECE), :],
            send_sem=z_send.at[p],
            recv_sem=z_recv.at[p],
            device_id=plane(-OFFSETS[p]),
            device_id_type=MESH,
        )

    edges = (
        (0, 1, (0, -1), 0), (0, 2, (0, 1), 0), (2, 3, (-1, 0), 0), (2, 4, (1, 0), 0), (3, 5, (-1, 0), 1), (4, 5, (1, 0), 2),
        (0, 6, None, 0), (1, 7, None, 0), (3, 8, None, 0),
    )

    def t_copy(e, n):
        source, target, way, part = edges[e]
        first, amount = STEPS[n][0] * PIECE, STEPS[n][1] * PIECE
        if part:
            amount //= 2
            first += amount * (part - 1)
        where = chip(0, 0, True) if way is None else chip(way[0], way[1], False)
        return pltpu.make_async_remote_copy(
            src_ref=slots.at[source, pl.ds(first, amount), :],
            dst_ref=slots.at[target, pl.ds(first, amount), :],
            send_sem=t_send.at[e, n],
            recv_sem=t_recv.at[e, n],
            device_id=where,
            device_id_type=MESH,
        )

    def prepare():
        def offset_of(slot):
            du, dv = COVER[slot] if slot < 6 else COVER[SIBLING[slot - 6]][::-1]
            nu, nv = (u + du + 4) % 4, (v + dv + 4) % 4
            nx = jnp.where(flip, nv, nu)
            ny = jnp.where(flip, nu, nv)
            nc = c if slot < 6 else 1 - c
            return nx * 512 + ny * 128 + nc * 64

        def steps_before(p):
            return ((z + OFFSETS[p] + 8) % 8) * 2048

        for slot in range(6):
            start = offset_of(slot)
            for p in range(8):
                position = (start + steps_before(p)) + lax.broadcasted_iota(jnp.int32, (PIECE, 128), 0)
                ids = jnp.zeros((PIECE, 128), jnp.int32)
                for m in range(1, 8):
                    ids += jnp.where(position >= bound_ref[m : m + 1, :], 1, 0)
                idr[slot, p * PIECE : (p + 1) * PIECE, :] = ids
        for slot in (0, 2, 3, 4, 5, 6, 7, 8):
            start = offset_of(slot)
            for q in range(4):
                lane = lax.broadcasted_iota(jnp.int32, (8, 128), 1)
                position = jnp.where(lane < 64, start + steps_before(2 * q) + lane, start + steps_before(2 * q + 1) + lane - 64)
                ids = jnp.zeros((8, 128), jnp.int32)
                for m in range(1, 8):
                    ids += jnp.where(position >= bound_ref[m : m + 1, :], 1, 0)
                idc[slot, :, q * 128 : (q + 1) * 128] = ids
        rowacc[...] = jnp.full(rowacc.shape, -1.0, jnp.float32)
        colacc[...] = jnp.full(colacc.shape, -1.0, jnp.float32)

    def quadrant(i, j, a, b, diagonal):
        rows = pl.ds(pl.multiple_of(a * 256, 256), 256)
        cols = pl.ds(pl.multiple_of(b * 256, 256), 256)
        scores = lax.dot_general(
            slots[i, rows, :], slots[j, cols, :], (((1,), (1,)), ((), ())), preferred_element_type=jnp.float32
        )
        best = rowacc[i, rows, :]
        for m in range(2):
            part = scores[:, m * 128 : (m + 1) * 128]
            their = idc[j, 0:1, pl.ds(pl.multiple_of(b * 256 + m * 128, 128), 128)]
            keep = idr[i, rows, :] == their
            if diagonal:
                row = lax.broadcasted_iota(jnp.int32, (256, 128), 0)
                col = lax.broadcasted_iota(jnp.int32, (256, 128), 1) + m * 128
                keep = jnp.logical_and(keep, row != col)
            part = jnp.where(keep, part, -1.0)
            best = jnp.maximum(best, part)
            at = pl.ds(pl.multiple_of(b * 256 + m * 128, 128), 128)
            colacc[j, :, at] = jnp.maximum(colacc[j, :, at], jnp.max(part.reshape(32, 8, 128), axis=0))
        rowacc[i, rows, :] = best

    which = (v // 2, u // 2, c)

    def early():
        def body(n, carry):
            quadrant(pick(n, [a for a, _ in FULL]), pick(n, [b for _, b in FULL]), 0, 0, False)
            return carry

        lax.fori_loop(0, len(FULL), body, 0)
        quadrant(0, 0, 0, 0, True)

    def late():
        def full(n, carry):
            i, j = pick(n, [a for a, _ in FULL]), pick(n, [b for _, b in FULL])
            for a, b in ((0, 1), (1, 0), (1, 1)):
                quadrant(i, j, a, b, False)
            return carry

        def half(n, carry):
            i, j = pick(n, [a for a, _, _ in HALF]), pick(n, [b for _, b, _ in HALF])
            quadrant(i, j, 0, 1, False)
            kind = pick(n, [k for _, _, k in HALF])
            h = jnp.where(kind == 0, which[0], jnp.where(kind == 1, which[1], which[2]))
            quadrant(i, j, h, h, False)
            return carry

        lax.fori_loop(0, len(FULL), full, 0)
        lax.fori_loop(0, len(HALF), half, 0)
        quadrant(0, 0, 0, 1, False)
        quadrant(0, 0, 1, 1, True)

    last = len(STEPS)
    for p in SENT[0]:
        z_copy(p).start()
    for tick in range(last + 3):
        if tick < last:
            first, amount = STEPS[tick]
            for p in range(max(first, 1), first + amount):
                z_copy(p).wait_recv()
            for e in (0, 1, 6):
                t_copy(e, tick).start()
            for p in SENT[tick + 1]:
                z_copy(p).start()
        if tick == 0:
            prepare()
        if 1 <= tick <= last:
            t_copy(1, tick - 1).wait_recv()
            t_copy(2, tick - 1).start()
            t_copy(3, tick - 1).start()
            t_copy(0, tick - 1).wait_recv()
            t_copy(7, tick - 1).start()
        if 2 <= tick <= last + 1:
            t_copy(2, tick - 2).wait_recv()
            t_copy(4, tick - 2).start()
            t_copy(8, tick - 2).start()
            t_copy(3, tick - 2).wait_recv()
            t_copy(5, tick - 2).start()
        if tick >= 3:
            for e in (4, 5, 6, 7, 8):
                t_copy(e, tick - 3).wait_recv()
        if tick == 5:
            early()
    late()

    for slot in range(9):
        best = jnp.max(colacc[slot], axis=0, keepdims=True)
        if slot < 6:
            best = jnp.maximum(best, jnp.max(rowacc[slot].T, axis=0, keepdims=True))
        res[slot] = best

    def r_copy(slot):
        du, dv = COVER[slot] if slot < 6 else COVER[SIBLING[slot - 6]][::-1]
        return pltpu.make_async_remote_copy(
            src_ref=res.at[slot],
            dst_ref=inb.at[slot],
            send_sem=r_send.at[slot],
            recv_sem=r_recv.at[slot],
            device_id=chip(du, dv, slot >= 6),
            device_id_type=MESH,
        )

    for slot in range(1, 9):
        r_copy(slot).start()
    best = res[0]
    for slot in range(1, 9):
        r_copy(slot).wait_recv()
        best = jnp.maximum(best, inb[slot])
    for q in range(4):
        near[q] = best[:, q * 128 : (q + 1) * 128]

    def o_copy(p):
        return pltpu.make_async_remote_copy(
            src_ref=near.at[p // 2],
            dst_ref=obuf.at[p],
            send_sem=o_send.at[p],
            recv_sem=o_recv.at[p],
            device_id=plane(OFFSETS[p]),
            device_id_type=MESH,
        )

    for p in range(1, 8):
        o_copy(p).start()
    out_ref[z] = near[0][:, 0:PIECE]
    for p in range(1, 8):
        o_copy(p).wait_recv()
        k = (z - OFFSETS[p] + 8) % 8
        out_ref[k] = obuf[p][:, (p % 2) * PIECE : (p % 2 + 1) * PIECE]
    for p in range(1, 8):
        z_copy(p).wait_send()
        o_copy(p).wait_send()
    for slot in range(1, 9):
        r_copy(slot).wait_send()
    for e in range(len(edges)):
        for n in range(last):
            t_copy(e, n).wait_send()


def local(embeddings, cluster_ids):
    ids = cluster_ids[0]
    below = jnp.sum(ids[None, :] < jnp.arange(8, dtype=jnp.int32)[:, None], axis=1, dtype=jnp.int32)
    mine = jnp.arange(8, dtype=jnp.int32)[:, None] == lax.axis_index("group")
    table = lax.psum(jnp.where(mine, below[None, :], 0), ("group", "tile"))
    bounds = lax.dynamic_index_in_dim(table, lax.axis_index("tile") // 4, 0, keepdims=False)
    bounds = jnp.broadcast_to(bounds[:, None], (8, 128))
    dma = pltpu.SemaphoreType.DMA
    out = pl.pallas_call(
        kernel,
        out_shape=jax.ShapeDtypeStruct((8, 1, PIECE), jnp.float32),
        in_specs=[pl.BlockSpec(memory_space=pltpu.VMEM)] * 2,
        out_specs=pl.BlockSpec(memory_space=pltpu.VMEM),
        scratch_shapes=[
            pltpu.VMEM((8, PIECE, D), jnp.bfloat16),
            pltpu.VMEM((9, ROWS, D), jnp.bfloat16),
            pltpu.VMEM((6, ROWS, 128), jnp.int32),
            pltpu.VMEM((9, 8, ROWS), jnp.int32),
            pltpu.VMEM((6, ROWS, 128), jnp.float32),
            pltpu.VMEM((9, 8, ROWS), jnp.float32),
            pltpu.VMEM((9, 1, ROWS), jnp.float32),
            pltpu.VMEM((9, 1, ROWS), jnp.float32),
            pltpu.VMEM((4, 1, 128), jnp.float32),
            pltpu.VMEM((8, 1, 128), jnp.float32),
            dma((8,)), dma((8,)), dma((9, 5)), dma((9, 5)), dma((9,)), dma((9,)), dma((8,)), dma((8,)),
        ],
        compiler_params=pltpu.CompilerParams(
            collective_id=0, has_side_effects=True, vmem_limit_bytes=40 * 1024 * 1024
        ),
        cost_estimate=pl.CostEstimate(flops=2 * 17 * 512 * 512 * 768, bytes_accessed=1 << 20, transcendentals=0),
    )(embeddings, bounds)
    return out.reshape(1, ROWS)


def solution(mesh):
    in_specs = (P("group", "tile", None), P("group", "tile"))
    out_specs = P("group", "tile")
    return jax.shard_map(local, mesh=mesh, in_specs=in_specs, out_specs=out_specs, check_vma=False)
```

```python
import functools

import jax
import jax.numpy as jnp
from jax import lax
from jax.experimental import pallas as pl
from jax.experimental.pallas import tpu as pltpu
from jax.sharding import PartitionSpec as P

MESH = pl.DeviceIdType.MESH
D = 768
ROWS = 512
PIECE = 64

COVER = ((0, 0), (0, 1), (0, -1), (1, -1), (-1, -1), (2, -1))
SIBLING = (0, 1, 3)
OFFSETS = (0, 1, -1, 2, -2, 3, -3, 4)
FULL = ((0, 2), (0, 3), (0, 4), (2, 3), (2, 6), (4, 6), (4, 8), (1, 6), (0, 5), (5, 6), (5, 8))
HALF_FIRST = ((0, 6, 2), (3, 6, 2), (3, 8, 2))
HALF_LAST = ((1, 2, 0), (1, 3, 0), (1, 4, 0), (1, 7, 2), (1, 5, 0), (2, 5, 1))
EDGES = (
    (0, 1, (0, -1)), (0, 2, (0, 1)), (2, 3, (-1, 0)), (2, 4, (1, 0)), (3, 5, (-1, 0)), (4, 5, (1, 0)),
    (0, 6, None), (1, 7, None), (3, 8, None), (2, 0, (0, -1)), (2, 5, (2, 0)),
)
LAST = 7
DIRECT = 5


def pick(n, table):
    value = jnp.int32(table[0])
    for at in range(1, len(table)):
        value = jnp.where(n == at, jnp.int32(table[at]), value)
    return value


def kernel(
    x_ref, id_ref, out_ref,
    raw, unit, slots, idr, idc, rowacc, colacc, res, inb, near, obuf, count, total, spread, bound,
    x_sem, z_send, z_recv, t_send, t_recv, r_send, r_recv, o_send, o_recv,
    a_send, a_recv, b_send, b_recv, c_send, c_recv,
):
    group = lax.axis_index("group")
    tile = lax.axis_index("tile")
    y, c = group // 2, group % 2
    z, x = tile // 4, tile % 4
    flip = c == 1
    u = jnp.where(flip, y, x)
    v = jnp.where(flip, x, y)

    def place(du, dv):
        nu, nv = (u + du + 4) % 4, (v + dv + 4) % 4
        return jnp.where(flip, nv, nu), jnp.where(flip, nu, nv)

    def chip(du, dv, other, dz=0):
        nx, ny = place(du, dv)
        nc = 1 - c if other else c
        return {"group": ny * 2 + nc, "tile": ((z + dz + 8) % 8) * 4 + nx}

    def plane(dz):
        return {"group": group, "tile": ((z + dz + 8) % 8) * 4 + x}

    def input_copy(p):
        k = (z - OFFSETS[p] + 8) % 8
        rows = pl.ds(pl.multiple_of(k * PIECE, PIECE), PIECE)
        return pltpu.make_async_copy(x_ref.at[0, rows, :], raw.at[p], x_sem.at[p])

    for p in range(8):
        input_copy(p).start()

    barrier = pltpu.get_barrier_semaphore()
    partners = [plane(o) for o in range(1, 8)]
    partners += [chip(a, b, False) for a, b in ((0, 1), (0, -1), (1, 0), (-1, 0), (1, -1), (-1, 1), (-1, -1), (1, 1), (2, -1), (2, 1), (0, 2), (2, 0))]
    partners += [chip(a, b, True) for a, b in ((0, 0), (1, 0), (0, -1), (-1, 1))]
    partners += [chip(jnp.where(flip, -1, 0), jnp.where(flip, 0, 1), True), chip(jnp.where(flip, 2, 0), jnp.where(flip, 0, 2), True)]
    partners += [chip(0, 1, False, 4), chip(0, -1, False, 4)]
    for partner in partners:
        pl.semaphore_signal(barrier, inc=1, device_id=partner, device_id_type=MESH)

    def normalize(p):
        input_copy(p).wait()
        values = raw[p].astype(jnp.float32)
        size = jnp.sum(values * values, axis=1, keepdims=True) + 1e-06
        return (values * (1.0 / jnp.sqrt(size))).astype(jnp.bfloat16)

    slots[0, 0:PIECE, :] = normalize(0)
    for p in range(1, 8):
        unit[p] = normalize(p)
    for m in range(8):
        below = jnp.zeros((1, 128), jnp.float32)
        for q in range(4):
            below += jnp.where(id_ref[:, q * 128 : (q + 1) * 128] < m, 1.0, 0.0)
        count[z, m : m + 1, :] = below

    pl.semaphore_wait(barrier, len(partners))

    def z_copy(p):
        return pltpu.make_async_remote_copy(
            src_ref=unit.at[p],
            dst_ref=slots.at[2 if p == LAST else 0, pl.ds(p * PIECE, PIECE), :],
            send_sem=z_send.at[p],
            recv_sem=z_recv.at[p],
            device_id=chip(0, 1, False, -OFFSETS[p]) if p == LAST else plane(-OFFSETS[p]),
            device_id_type=MESH,
        )

    def t_copy(e, p):
        source, target, way = EDGES[e]
        first, amount = p * PIECE, PIECE
        return pltpu.make_async_remote_copy(
            src_ref=slots.at[source, pl.ds(first, amount), :],
            dst_ref=slots.at[target, pl.ds(first, amount), :],
            send_sem=t_send.at[e, p],
            recv_sem=t_recv.at[e, p],
            device_id=chip(0, 0, True) if way is None else chip(way[0], way[1], False),
            device_id_type=MESH,
        )

    def edges_of(p):
        if p == LAST:
            return (0, 2, 3, 6, 7, 8, 9, 10)
        return (0, 1, 2, 3, 10 if p >= DIRECT else 4 + p % 2, 6, 7, 8)

    def go(p, *edges):
        for e in edges:
            if e in edges_of(p):
                t_copy(e, p).start()

    def come(p, *edges):
        for e in edges:
            if e in edges_of(p):
                t_copy(e, p).wait_recv()

    def root(*pieces):
        for p in pieces:
            if p:
                z_copy(p).wait_recv()
            go(p, 0, 1, 6)

    def second(*pieces):
        for p in pieces:
            come(p, 1)
            go(p, 2, 3, 10)
            come(p, 0)
            go(p, 7)

    def third(*pieces):
        for p in pieces:
            come(p, 2)
            go(p, 4, 8)
            come(p, 3)
            go(p, 5)

    holder = group == z

    def a_copy(sender):
        return pltpu.make_async_remote_copy(
            src_ref=count.at[sender], dst_ref=count.at[sender], send_sem=a_send, recv_sem=a_recv.at[sender],
            device_id={"group": group, "tile": group * 4 + x}, device_id_type=MESH,
        )

    def b_copy(n):
        return pltpu.make_async_remote_copy(
            src_ref=total, dst_ref=spread.at[0], send_sem=b_send.at[n], recv_sem=b_recv,
            device_id={"group": (group + n) % 8, "tile": tile}, device_id_type=MESH,
        )

    def c_copy(n):
        return pltpu.make_async_remote_copy(
            src_ref=spread.at[0], dst_ref=spread.at[n], send_sem=c_send.at[n], recv_sem=c_recv.at[n],
            device_id={"group": group, "tile": z * 4 + (x + n) % 4}, device_id_type=MESH,
        )

    def bounds_a():
        @pl.when(jnp.logical_not(holder))
        def _():
            a_copy(z).start()

    def bounds_b():
        @pl.when(holder)
        def _():
            for n in range(1, 8):
                a_copy((z + n) % 8).wait_recv()
            value = count[0]
            for n in range(1, 8):
                value += count[n]
            total[...] = value
            spread[0] = value
            for n in range(1, 8):
                b_copy(n).start()

    def bounds_c():
        @pl.when(jnp.logical_not(holder))
        def _():
            b_copy(1).wait_recv()

        for n in range(1, 4):
            c_copy(n).start()

    def bounds_d():
        value = spread[0]
        for n in range(1, 4):
            c_copy(n).wait_recv()
            value += spread[n]
        bound[...] = jnp.broadcast_to(jnp.sum(value, axis=1, keepdims=True), (8, 128)).astype(jnp.int32)

    def bounds_end():
        @pl.when(jnp.logical_not(holder))
        def _():
            a_copy(z).wait_send()

        @pl.when(holder)
        def _():
            for n in range(1, 8):
                b_copy(n).wait_send()

        for n in range(1, 4):
            c_copy(n).wait_send()

    def identify():
        def offset_of(slot):
            nx, ny = place(*(COVER[slot] if slot < 6 else COVER[SIBLING[slot - 6]][::-1]))
            return nx * 512 + ny * 128 + (c if slot < 6 else 1 - c) * 64

        def steps_before(p):
            return ((z + OFFSETS[p] + 8) % 8) * 2048

        def cluster(position):
            ids = jnp.zeros(position.shape, jnp.int32)
            for m in range(1, 8):
                ids += jnp.where(position >= bound[m : m + 1, :], 1, 0)
            return ids

        for slot in range(6):
            start = offset_of(slot)
            for p in range(8):
                position = (start + steps_before(p)) + lax.broadcasted_iota(jnp.int32, (PIECE, 128), 0)
                idr[slot, p * PIECE : (p + 1) * PIECE, :] = cluster(position)
        for slot in (0, 2, 3, 4, 5, 6, 7, 8):
            start = offset_of(slot)
            for q in range(4):
                lane = lax.broadcasted_iota(jnp.int32, (8, 128), 1)
                position = jnp.where(lane < 64, start + steps_before(2 * q) + lane, start + steps_before(2 * q + 1) + lane - 64)
                idc[slot, :, q * 128 : (q + 1) * 128] = cluster(position)

    def clear():
        rowacc[...] = jnp.full(rowacc.shape, -1.0, jnp.float32)
        colacc[...] = jnp.full(colacc.shape, -1.0, jnp.float32)

    def score(i, j, rows, cols, diagonal=False):
        height = rows[1]
        rows = pl.ds(rows[0], height)
        scores = lax.dot_general(
            slots[i, rows, :], slots[j, pl.ds(cols[0], cols[1]), :], (((1,), (1,)), ((), ())),
            preferred_element_type=jnp.float32,
        )
        best = rowacc[i, rows, :]
        for m in range(cols[1] // 128):
            part = scores[:, m * 128 : (m + 1) * 128]
            at = cols[0] + m * 128
            at = pl.ds(at if isinstance(at, int) else pl.multiple_of(at, 128), 128)
            keep = idr[i, rows, :] == idc[j, 0:1, at]
            if diagonal:
                row = lax.broadcasted_iota(jnp.int32, (height, 128), 0)
                col = lax.broadcasted_iota(jnp.int32, (height, 128), 1) + m * 128
                keep = jnp.logical_and(keep, row != col)
            part = jnp.where(keep, part, -1.0)
            best = jnp.maximum(best, part)
            colacc[j, :, at] = jnp.maximum(colacc[j, :, at], jnp.max(part.reshape(height // 8, 8, 128), axis=0))
        rowacc[i, rows, :] = best

    def loop(table, body, together):
        def step(n, carry):
            for at in range(together):
                body([pick(n, column) for column in zip(*table[at::together])])
            return carry

        if len(table) == together:
            for entry in table:
                body(entry)
        else:
            lax.fori_loop(0, len(table) // together, step, 0)

    def early(entry):
        score(entry[0], entry[1], (0, 256), (0, 256))

    def late(entry):
        score(entry[0], entry[1], (0, 512), (256, 256))
        score(entry[0], entry[1], (256, 256), (0, 256))

    def half(entry):
        i, j, kind = entry
        h = jnp.where(kind == 0, v // 2, jnp.where(kind == 1, u // 2, c))
        h = pl.multiple_of(h * 256, 256)
        score(i, j, (0, 256), (256, 256))
        score(i, j, (h, 256), (h, 256))

    def settle(slot):
        best = jnp.max(colacc[slot], axis=0, keepdims=True) if slot != 1 else None
        if slot < 6:
            rows = jnp.max(rowacc[slot].T, axis=0, keepdims=True)
            best = rows if best is None else jnp.maximum(best, rows)
        res[slot] = best

    def r_copy(slot):
        du, dv = COVER[slot] if slot < 6 else COVER[SIBLING[slot - 6]][::-1]
        return pltpu.make_async_remote_copy(
            src_ref=res.at[slot], dst_ref=inb.at[slot], send_sem=r_send.at[slot], recv_sem=r_recv.at[slot],
            device_id=chip(du, dv, slot >= 6), device_id_type=MESH,
        )

    def answer(*chosen):
        for slot in chosen:
            settle(slot)
            r_copy(slot).start()

    z_copy(1).start()
    z_copy(2).start()
    root(0)
    z_copy(3).start()
    z_copy(4).start()
    bounds_a()
    clear()
    second(0)
    root(1, 2)
    z_copy(5).start()
    z_copy(6).start()
    third(0)
    bounds_b()
    second(1, 2)
    root(3, 4)
    z_copy(LAST).start()
    third(1, 2)
    bounds_c()
    second(3, 4)
    bounds_d()
    identify()
    root(5, 6)
    third(3, 4)
    for p in range(4):
        come(p, 6, 7, 8)
    loop(FULL[:8], early, 4)
    second(5, 6)
    z_copy(LAST).wait_recv()
    go(LAST, 2, 3, 9, 10)
    for p in range(4):
        come(p, 4, 5)
    loop(FULL[8:], early, 3)
    score(0, 0, (0, 256), (0, 256), True)
    third(5, 6)
    come(LAST, 9)
    go(LAST, 0, 6)
    third(LAST)
    loop(FULL[:4], late, 4)
    score(0, 0, (0, 256), (256, 256))
    score(0, 0, (256, 256), (256, 256), True)
    for p in range(4, 7):
        come(p, 6, 8)
    come(LAST, 6, 8)
    loop(FULL[4:7], late, 3)
    loop(HALF_FIRST, half, 3)
    come(LAST, 0)
    go(LAST, 7)
    loop(FULL[7:8], late, 1)
    loop(HALF_LAST[:3], half, 3)
    answer(3, 4)
    for p in range(4, 8):
        come(p, 7)
    loop(HALF_LAST[3:4], half, 1)
    answer(7)
    for p in range(4, 8):
        come(p, 4, 5, 10)
    loop(FULL[8:], late, 3)
    loop(HALF_LAST[4:], half, 2)
    answer(5, 1, 2, 6, 8)
    settle(0)
    bounds_end()
    for p in range(8):
        if p:
            z_copy(p).wait_send()
        for e in edges_of(p):
            t_copy(e, p).wait_send()

    best = res[0]
    for slot in (3, 4, 7, 5, 1, 2, 6, 8):
        r_copy(slot).wait_recv()
        best = jnp.maximum(best, inb[slot])
    lane = lax.broadcasted_iota(jnp.int32, (1, 128), 1)
    for p in range(8):
        part = best[:, p // 2 * 128 : (p // 2 + 1) * 128]
        turned = pltpu.roll(part, 64, 1)
        near[p] = jnp.where((lane < 64) == (p % 2 == 0), part, turned)

    def o_copy(p):
        return pltpu.make_async_remote_copy(
            src_ref=near.at[p], dst_ref=obuf.at[z], send_sem=o_send.at[p], recv_sem=o_recv.at[p],
            device_id=plane(OFFSETS[p]), device_id_type=MESH,
        )

    for p in (7, 5, 6, 3, 4, 1, 2):
        o_copy(p).start()
    obuf[z] = near[0]
    for slot in range(1, 9):
        r_copy(slot).wait_send()
    for p in (1, 2, 3, 4, 5, 6, 7):
        o_copy(p).wait_recv()
    for q in range(4):
        out_ref[:, q * 128 : (q + 1) * 128] = jnp.where(lane < 64, obuf[2 * q], obuf[2 * q + 1])
    for p in range(1, 8):
        o_copy(p).wait_send()


def local(embeddings, cluster_ids):
    dma = pltpu.SemaphoreType.DMA
    return pl.pallas_call(
        kernel,
        out_shape=jax.ShapeDtypeStruct((1, ROWS), jnp.float32),
        in_specs=[pl.BlockSpec(memory_space=pl.ANY), pl.BlockSpec(memory_space=pltpu.VMEM)],
        out_specs=pl.BlockSpec(memory_space=pltpu.VMEM),
        scratch_shapes=[
            pltpu.VMEM((8, PIECE, D), jnp.bfloat16),
            pltpu.VMEM((8, PIECE, D), jnp.bfloat16),
            pltpu.VMEM((9, ROWS, D), jnp.bfloat16),
            pltpu.VMEM((6, ROWS, 128), jnp.int32),
            pltpu.VMEM((9, 8, ROWS), jnp.int32),
            pltpu.VMEM((6, ROWS, 128), jnp.float32),
            pltpu.VMEM((9, 8, ROWS), jnp.float32),
            pltpu.VMEM((9, 1, ROWS), jnp.float32),
            pltpu.VMEM((9, 1, ROWS), jnp.float32),
            pltpu.VMEM((8, 1, 128), jnp.float32),
            pltpu.VMEM((8, 1, 128), jnp.float32),
            pltpu.VMEM((8, 8, 128), jnp.float32),
            pltpu.VMEM((8, 128), jnp.float32),
            pltpu.VMEM((4, 8, 128), jnp.float32),
            pltpu.VMEM((8, 128), jnp.int32),
            dma((8,)), dma((8,)), dma((8,)), dma((11, 8)), dma((11, 8)), dma((9,)), dma((9,)), dma((8,)), dma((8,)),
            dma, dma((8,)), dma((8,)), dma, dma((4,)), dma((4,)),
        ],
        compiler_params=pltpu.CompilerParams(
            collective_id=0, has_side_effects=True, vmem_limit_bytes=40 * 1024 * 1024
        ),
        cost_estimate=pl.CostEstimate(flops=2 * 17 * 512 * 512 * 768, bytes_accessed=1 << 20, transcendentals=0),
    )(embeddings, cluster_ids)


def solution(mesh):
    in_specs = (P("group", "tile", None), P("group", "tile"))
    out_specs = P("group", "tile")
    return jax.shard_map(local, mesh=mesh, in_specs=in_specs, out_specs=out_specs, check_vma=False)
```

```python
import functools

import jax
import jax.numpy as jnp
from jax import lax
from jax.experimental import pallas as pl
from jax.experimental.pallas import tpu as pltpu
from jax.sharding import PartitionSpec as P

MESH = pl.DeviceIdType.MESH
D = 768
ROWS = 512
PIECE = 64

COVER = ((0, 0), (0, 1), (0, -1), (1, -1), (-1, -1), (2, -1))
SIBLING = (0, 1, 3)
OFFSETS = (0, 1, -1, 2, -2, 3, -3, 4)
FULL = ((0, 2), (0, 3), (0, 4), (2, 3), (2, 6), (1, 6), (4, 6), (4, 8), (0, 5), (5, 6), (5, 8))
HALF = ((1, 2, 0), (1, 3, 0), (1, 4, 0), (0, 6, 2), (3, 6, 2), (3, 8, 2), (1, 7, 2), (1, 5, 0), (2, 5, 1))
EDGES = (
    (0, 1, (0, -1)), (0, 2, (0, 1)), (2, 3, (-1, 0)), (2, 4, (1, 0)), (3, 5, (-1, 0)), (4, 5, (1, 0)),
    (0, 6, None), (1, 7, None), (3, 8, None), (2, 5, (2, 0)),
)
DIRECT = 7


def pick(n, table):
    value = jnp.int32(table[0])
    for at in range(1, len(table)):
        value = jnp.where(n == at, jnp.int32(table[at]), value)
    return value


def kernel(
    x_ref, id_ref, out_ref,
    raw, unit, slots, idr, idc, rowacc, colacc, res, inb, near, obuf, count, total, spread, bound,
    x_sem, z_send, z_recv, t_send, t_recv, r_send, r_recv, o_send, o_recv,
    a_send, a_recv, b_send, b_recv, c_send, c_recv,
):
    group = lax.axis_index("group")
    tile = lax.axis_index("tile")
    y, c = group // 2, group % 2
    z, x = tile // 4, tile % 4
    flip = c == 1
    u = jnp.where(flip, y, x)
    v = jnp.where(flip, x, y)

    def place(du, dv):
        nu, nv = (u + du + 4) % 4, (v + dv + 4) % 4
        return jnp.where(flip, nv, nu), jnp.where(flip, nu, nv)

    def chip(du, dv, other, dz=0):
        nx, ny = place(du, dv)
        nc = 1 - c if other else c
        return {"group": ny * 2 + nc, "tile": ((z + dz + 8) % 8) * 4 + nx}

    def plane(dz):
        return {"group": group, "tile": ((z + dz + 8) % 8) * 4 + x}

    def input_copy(p):
        k = (z - OFFSETS[p] + 8) % 8
        rows = pl.ds(pl.multiple_of(k * PIECE, PIECE), PIECE)
        return pltpu.make_async_copy(x_ref.at[0, rows, :], raw.at[p], x_sem.at[p])

    for p in range(8):
        input_copy(p).start()

    barrier = pltpu.get_barrier_semaphore()
    partners = [plane(o) for o in range(1, 8)]
    partners += [chip(a, b, False) for a, b in ((0, 1), (0, -1), (1, 0), (-1, 0), (1, -1), (-1, 1), (-1, -1), (1, 1), (2, -1), (2, 1), (0, 2), (2, 0))]
    partners += [chip(a, b, True) for a, b in ((0, 0), (1, 0), (0, -1), (-1, 1))]
    partners += [chip(jnp.where(flip, -1, 0), jnp.where(flip, 0, 1), True), chip(jnp.where(flip, 2, 0), jnp.where(flip, 0, 2), True)]
    for partner in partners:
        pl.semaphore_signal(barrier, inc=1, device_id=partner, device_id_type=MESH)

    def normalize(p):
        input_copy(p).wait()
        values = raw[p].astype(jnp.float32)
        size = jnp.sum(values * values, axis=1, keepdims=True) + 1e-06
        return (values * (1.0 / jnp.sqrt(size))).astype(jnp.bfloat16)

    slots[0, 0:PIECE, :] = normalize(0)
    for p in range(1, 8):
        unit[p] = normalize(p)
    for m in range(8):
        below = jnp.zeros((1, 128), jnp.float32)
        for q in range(4):
            below += jnp.where(id_ref[:, q * 128 : (q + 1) * 128] < m, 1.0, 0.0)
        count[z, m : m + 1, :] = below

    pl.semaphore_wait(barrier, len(partners))

    def z_copy(p):
        return pltpu.make_async_remote_copy(
            src_ref=unit.at[p],
            dst_ref=slots.at[0, pl.ds(p * PIECE, PIECE), :],
            send_sem=z_send.at[p],
            recv_sem=z_recv.at[p],
            device_id=plane(-OFFSETS[p]),
            device_id_type=MESH,
        )

    def t_copy(e, p):
        source, target, way = EDGES[e]
        first, amount = p * PIECE, PIECE
        return pltpu.make_async_remote_copy(
            src_ref=slots.at[source, pl.ds(first, amount), :],
            dst_ref=slots.at[target, pl.ds(first, amount), :],
            send_sem=t_send.at[e, p],
            recv_sem=t_recv.at[e, p],
            device_id=chip(0, 0, True) if way is None else chip(way[0], way[1], False),
            device_id_type=MESH,
        )

    def edges_of(p):
        return (0, 1, 2, 3, 9 if p >= DIRECT else 4 + p % 2, 6, 7, 8)

    def go(p, *edges):
        for e in edges:
            if e in edges_of(p):
                t_copy(e, p).start()

    def come(p, *edges):
        for e in edges:
            if e in edges_of(p):
                t_copy(e, p).wait_recv()

    def root(p):
        if p:
            z_copy(p).wait_recv()
        go(p, 1, 0, 6)

    def into2(p):
        come(p, 1)
        go(p, 2, 3, 9)

    def into1(p):
        come(p, 0)
        go(p, 7)

    def into3(p):
        come(p, 2)
        go(p, 4, 8)

    def into4(p):
        come(p, 3)
        go(p, 5)

    holder = group == z

    def a_copy(sender):
        return pltpu.make_async_remote_copy(
            src_ref=count.at[sender], dst_ref=count.at[sender], send_sem=a_send, recv_sem=a_recv.at[sender],
            device_id={"group": group, "tile": group * 4 + x}, device_id_type=MESH,
        )

    def b_copy(n):
        return pltpu.make_async_remote_copy(
            src_ref=total, dst_ref=spread.at[0], send_sem=b_send.at[n], recv_sem=b_recv,
            device_id={"group": (group + n) % 8, "tile": tile}, device_id_type=MESH,
        )

    def c_copy(n):
        return pltpu.make_async_remote_copy(
            src_ref=spread.at[0], dst_ref=spread.at[n], send_sem=c_send.at[n], recv_sem=c_recv.at[n],
            device_id={"group": group, "tile": z * 4 + (x + n) % 4}, device_id_type=MESH,
        )

    def bounds_a():
        @pl.when(jnp.logical_not(holder))
        def _():
            a_copy(z).start()

    def bounds_b():
        @pl.when(holder)
        def _():
            for n in range(1, 8):
                a_copy((z + n) % 8).wait_recv()
            value = count[0]
            for n in range(1, 8):
                value += count[n]
            total[...] = value
            spread[0] = value
            for n in range(1, 8):
                b_copy(n).start()

    def bounds_c():
        @pl.when(jnp.logical_not(holder))
        def _():
            b_copy(1).wait_recv()

        for n in range(1, 4):
            c_copy(n).start()

    def bounds_d():
        value = spread[0]
        for n in range(1, 4):
            c_copy(n).wait_recv()
            value += spread[n]
        bound[...] = jnp.broadcast_to(jnp.sum(value, axis=1, keepdims=True), (8, 128)).astype(jnp.int32)

    def bounds_end():
        @pl.when(jnp.logical_not(holder))
        def _():
            a_copy(z).wait_send()

        @pl.when(holder)
        def _():
            for n in range(1, 8):
                b_copy(n).wait_send()

        for n in range(1, 4):
            c_copy(n).wait_send()

    def identify(rows, cols):
        def offset_of(slot):
            nx, ny = place(*(COVER[slot] if slot < 6 else COVER[SIBLING[slot - 6]][::-1]))
            return nx * 512 + ny * 128 + (c if slot < 6 else 1 - c) * 64

        def steps_before(p):
            return ((z + OFFSETS[p] + 8) % 8) * 2048

        def cluster(position):
            ids = jnp.zeros(position.shape, jnp.int32)
            for m in range(1, 8):
                ids += jnp.where(position >= bound[m : m + 1, :], 1, 0)
            return ids

        for slot in rows:
            start = offset_of(slot)
            for p in range(8):
                position = (start + steps_before(p)) + lax.broadcasted_iota(jnp.int32, (PIECE, 128), 0)
                idr[slot, p * PIECE : (p + 1) * PIECE, :] = cluster(position)
        for slot in cols:
            start = offset_of(slot)
            for q in range(4):
                lane = lax.broadcasted_iota(jnp.int32, (8, 128), 1)
                position = jnp.where(lane < 64, start + steps_before(2 * q) + lane, start + steps_before(2 * q + 1) + lane - 64)
                idc[slot, :, q * 128 : (q + 1) * 128] = cluster(position)

    def clear():
        rowacc[...] = jnp.full(rowacc.shape, -1.0, jnp.float32)
        colacc[...] = jnp.full(colacc.shape, -1.0, jnp.float32)

    def score(i, j, rows, cols, diagonal=False):
        height = rows[1]
        rows = pl.ds(rows[0], height)
        scores = lax.dot_general(
            slots[i, rows, :], slots[j, pl.ds(cols[0], cols[1]), :], (((1,), (1,)), ((), ())),
            preferred_element_type=jnp.float32,
        )
        best = rowacc[i, rows, :]
        for m in range(cols[1] // 128):
            part = scores[:, m * 128 : (m + 1) * 128]
            at = cols[0] + m * 128
            at = pl.ds(at if isinstance(at, int) else pl.multiple_of(at, 128), 128)
            keep = idr[i, rows, :] == idc[j, 0:1, at]
            if diagonal:
                row = lax.broadcasted_iota(jnp.int32, (height, 128), 0)
                col = lax.broadcasted_iota(jnp.int32, (height, 128), 1) + m * 128
                keep = jnp.logical_and(keep, row != col)
            part = jnp.where(keep, part, -1.0)
            best = jnp.maximum(best, part)
            colacc[j, :, at] = jnp.maximum(colacc[j, :, at], jnp.max(part.reshape(height // 8, 8, 128), axis=0))
        rowacc[i, rows, :] = best

    def loop(table, body, together):
        def step(n, carry):
            for at in range(together):
                body([pick(n, column) for column in zip(*table[at::together])])
            return carry

        if len(table) == together:
            for entry in table:
                body(entry)
        else:
            lax.fori_loop(0, len(table) // together, step, 0)

    def early(entry):
        score(entry[0], entry[1], (0, 256), (0, 256))

    def late(entry):
        score(entry[0], entry[1], (0, 512), (256, 256))
        score(entry[0], entry[1], (256, 256), (0, 256))

    def half(entry):
        i, j, kind = entry
        h = jnp.where(kind == 0, v // 2, jnp.where(kind == 1, u // 2, c))
        h = pl.multiple_of(h * 256, 256)
        score(i, j, (0, 256), (256, 256))
        score(i, j, (h, 256), (h, 256))

    def settle(slot):
        best = jnp.max(colacc[slot], axis=0, keepdims=True) if slot != 1 else None
        if slot < 6:
            rows = jnp.max(rowacc[slot].T, axis=0, keepdims=True)
            best = rows if best is None else jnp.maximum(best, rows)
        res[slot] = best

    def r_copy(slot):
        du, dv = COVER[slot] if slot < 6 else COVER[SIBLING[slot - 6]][::-1]
        return pltpu.make_async_remote_copy(
            src_ref=res.at[slot], dst_ref=inb.at[slot], send_sem=r_send.at[slot], recv_sem=r_recv.at[slot],
            device_id=chip(du, dv, slot >= 6), device_id_type=MESH,
        )

    def answer(*chosen):
        for slot in chosen:
            settle(slot)
            r_copy(slot).start()

    bounds_a()
    for p in range(1, 3):
        z_copy(p).start()
    root(0)
    for p in range(3, 8):
        z_copy(p).start()
    clear()
    root(1)
    root(2)
    bounds_b()
    into2(0)
    into1(0)
    root(3)
    into2(1)
    into1(1)
    root(4)
    into2(2)
    into1(2)
    into3(0)
    into4(0)
    root(5)
    into2(3)
    into1(3)
    bounds_c()
    into3(1)
    into4(1)
    root(6)
    into2(4)
    into1(4)
    into3(2)
    into4(2)
    root(7)
    into2(5)
    into4(3)
    into3(3)
    bounds_d()
    identify((0, 1, 2), ())
    into2(6)
    into1(5)
    into3(4)
    into4(4)
    identify((3, 4, 5), ())
    identify((), (0, 2, 3, 4, 5, 6, 7, 8))
    into2(7)
    into4(5)
    loop(FULL[:4], early, 4)
    into1(7)
    loop(FULL[:1], late, 1)
    into1(6)
    into3(6)
    into3(5)
    for p in range(4):
        come(p, 4, 5)
    loop(FULL[8:9], early, 1)
    score(0, 0, (0, 256), (0, 256), True)
    into4(6)
    for p in range(4):
        come(p, 6, 8)
    loop(FULL[4:8], early, 4)
    loop(FULL[9:], early, 2)
    for p in range(4, 8):
        come(p, 6)
    loop(FULL[4:6], late, 2)
    loop(HALF[3:4], half, 1)
    into4(7)
    loop(HALF[:1], half, 1)
    score(0, 0, (0, 256), (256, 256))
    score(0, 0, (256, 256), (256, 256), True)
    into3(7)
    loop(FULL[1:4], late, 3)
    loop(FULL[6:7], late, 1)
    loop(HALF[1:3], half, 2)
    loop(HALF[4:5], half, 1)
    for p in range(4, 8):
        come(p, 8)
    loop(FULL[7:8], late, 1)
    for p in range(8):
        come(p, 7)
    loop(HALF[5:7], half, 2)
    answer(3, 4, 7)
    for p in range(4, 8):
        come(p, 4, 5, 9)
    loop(FULL[8:], late, 3)
    loop(HALF[7:], half, 2)
    answer(5, 1, 2, 6, 8)
    settle(0)
    bounds_end()
    for p in range(8):
        if p:
            z_copy(p).wait_send()
        for e in edges_of(p):
            t_copy(e, p).wait_send()

    best = res[0]
    for slot in (3, 4, 7, 5, 1, 2, 6, 8):
        r_copy(slot).wait_recv()
        best = jnp.maximum(best, inb[slot])
    lane = lax.broadcasted_iota(jnp.int32, (1, 128), 1)
    for p in range(8):
        part = best[:, p // 2 * 128 : (p // 2 + 1) * 128]
        turned = pltpu.roll(part, 64, 1)
        near[p] = jnp.where((lane < 64) == (p % 2 == 0), part, turned)

    def o_copy(p):
        return pltpu.make_async_remote_copy(
            src_ref=near.at[p], dst_ref=obuf.at[z], send_sem=o_send.at[p], recv_sem=o_recv.at[p],
            device_id=plane(OFFSETS[p]), device_id_type=MESH,
        )

    for p in (7, 5, 6, 3, 4, 1, 2):
        o_copy(p).start()
    obuf[z] = near[0]
    for slot in range(1, 9):
        r_copy(slot).wait_send()
    for p in (1, 2, 3, 4, 5, 6, 7):
        o_copy(p).wait_recv()
    for q in range(4):
        out_ref[:, q * 128 : (q + 1) * 128] = jnp.where(lane < 64, obuf[2 * q], obuf[2 * q + 1])
    for p in range(1, 8):
        o_copy(p).wait_send()


def local(embeddings, cluster_ids):
    dma = pltpu.SemaphoreType.DMA
    return pl.pallas_call(
        kernel,
        out_shape=jax.ShapeDtypeStruct((1, ROWS), jnp.float32),
        in_specs=[pl.BlockSpec(memory_space=pl.ANY), pl.BlockSpec(memory_space=pltpu.VMEM)],
        out_specs=pl.BlockSpec(memory_space=pltpu.VMEM),
        scratch_shapes=[
            pltpu.VMEM((8, PIECE, D), jnp.bfloat16),
            pltpu.VMEM((8, PIECE, D), jnp.bfloat16),
            pltpu.VMEM((9, ROWS, D), jnp.bfloat16),
            pltpu.VMEM((6, ROWS, 128), jnp.int32),
            pltpu.VMEM((9, 8, ROWS), jnp.int32),
            pltpu.VMEM((6, ROWS, 128), jnp.float32),
            pltpu.VMEM((9, 8, ROWS), jnp.float32),
            pltpu.VMEM((9, 1, ROWS), jnp.float32),
            pltpu.VMEM((9, 1, ROWS), jnp.float32),
            pltpu.VMEM((8, 1, 128), jnp.float32),
            pltpu.VMEM((8, 1, 128), jnp.float32),
            pltpu.VMEM((8, 8, 128), jnp.float32),
            pltpu.VMEM((8, 128), jnp.float32),
            pltpu.VMEM((4, 8, 128), jnp.float32),
            pltpu.VMEM((8, 128), jnp.int32),
            dma((8,)), dma((8,)), dma((8,)), dma((10, 8)), dma((10, 8)), dma((9,)), dma((9,)), dma((8,)), dma((8,)),
            dma, dma((8,)), dma((8,)), dma, dma((4,)), dma((4,)),
        ],
        compiler_params=pltpu.CompilerParams(
            collective_id=0, has_side_effects=True, vmem_limit_bytes=40 * 1024 * 1024
        ),
        cost_estimate=pl.CostEstimate(flops=2 * 17 * 512 * 512 * 768, bytes_accessed=1 << 20, transcendentals=0),
    )(embeddings, cluster_ids)


def solution(mesh):
    in_specs = (P("group", "tile", None), P("group", "tile"))
    out_specs = P("group", "tile")
    return jax.shard_map(local, mesh=mesh, in_specs=in_specs, out_specs=out_specs, check_vma=False)
```

```python
import functools

import jax
import jax.numpy as jnp
from jax import lax
from jax.experimental import pallas as pl
from jax.experimental.pallas import tpu as pltpu
from jax.sharding import PartitionSpec as P

MESH = pl.DeviceIdType.MESH
D = 768
ROWS = 512
PIECE = 64

COVER = ((0, 0), (0, 1), (0, -1), (1, -1), (-1, -1), (2, -1))
SIBLING = (0, 1, 3)
OFFSETS = (0, 1, -1, 2, -2, 3, -3, 4)
FULL = ((0, 2), (0, 3), (2, 3), (0, 4), (2, 6), (1, 6), (4, 6), (4, 8), (5, 0), (5, 6), (5, 8))
HALF = ((1, 2, 0), (1, 4, 0), (0, 6, 2), (1, 3, 0), (3, 6, 2), (3, 8, 2), (1, 7, 2), (5, 1, 0), (5, 2, 1))
EDGES = (
    (0, 1, (0, -1)), (0, 2, (0, 1)), (2, 3, (-1, 0)), (2, 4, (1, 0)), (3, 5, (-1, 0)), (4, 5, (1, 0)),
    (0, 6, None), (1, 7, None), (3, 8, None),
)


def pick(n, table):
    value = jnp.int32(table[0])
    for at in range(1, len(table)):
        value = jnp.where(n == at, jnp.int32(table[at]), value)
    return value


def kernel(
    x_ref, id_ref, out_ref,
    raw, unit, slots, idr, idc, rowacc, colacc, res, inb, near, obuf, count, total, spread, bound,
    x_sem, z_send, z_recv, t_send, t_recv, r_send, r_recv, o_send, o_recv,
    a_send, a_recv, b_send, b_recv, c_send, c_recv,
):
    group = lax.axis_index("group")
    tile = lax.axis_index("tile")
    y, c = group // 2, group % 2
    z, x = tile // 4, tile % 4
    flip = c == 1
    u = jnp.where(flip, y, x)
    v = jnp.where(flip, x, y)

    def place(du, dv):
        nu, nv = (u + du + 4) % 4, (v + dv + 4) % 4
        return jnp.where(flip, nv, nu), jnp.where(flip, nu, nv)

    def chip(du, dv, other, dz=0):
        nx, ny = place(du, dv)
        nc = 1 - c if other else c
        return {"group": ny * 2 + nc, "tile": ((z + dz + 8) % 8) * 4 + nx}

    def plane(dz):
        return {"group": group, "tile": ((z + dz + 8) % 8) * 4 + x}

    def input_copy(p):
        k = (z - OFFSETS[p] + 8) % 8
        rows = pl.ds(pl.multiple_of(k * PIECE, PIECE), PIECE)
        return pltpu.make_async_copy(x_ref.at[0, rows, :], raw.at[p], x_sem.at[p])

    for p in range(8):
        input_copy(p).start()

    barrier = pltpu.get_barrier_semaphore()
    partners = [plane(o) for o in range(1, 8)]
    partners += [chip(a, b, False) for a, b in ((0, 1), (0, -1), (1, 0), (-1, 0), (1, -1), (-1, 1), (-1, -1), (1, 1), (2, -1), (2, 1), (0, 2), (2, 0))]
    partners += [chip(a, b, True) for a, b in ((0, 0), (1, 0), (0, -1), (-1, 1))]
    partners += [chip(jnp.where(flip, -1, 0), jnp.where(flip, 0, 1), True), chip(jnp.where(flip, 2, 0), jnp.where(flip, 0, 2), True)]
    for partner in partners:
        pl.semaphore_signal(barrier, inc=1, device_id=partner, device_id_type=MESH)

    def normalize(p):
        input_copy(p).wait()
        values = raw[p].astype(jnp.float32)
        size = jnp.sum(values * values, axis=1, keepdims=True) + 1e-06
        return (values * (1.0 / jnp.sqrt(size))).astype(jnp.bfloat16)

    slots[0, 0:PIECE, :] = normalize(0)
    for p in range(1, 8):
        unit[p] = normalize(p)
    for m in range(8):
        below = jnp.zeros((1, 128), jnp.float32)
        for q in range(4):
            below += jnp.where(id_ref[:, q * 128 : (q + 1) * 128] < m, 1.0, 0.0)
        count[z, m : m + 1, :] = below

    pl.semaphore_wait(barrier, len(partners))

    def z_copy(p):
        return pltpu.make_async_remote_copy(
            src_ref=unit.at[p],
            dst_ref=slots.at[0, pl.ds(p * PIECE, PIECE), :],
            send_sem=z_send.at[p],
            recv_sem=z_recv.at[p],
            device_id=plane(-OFFSETS[p]),
            device_id_type=MESH,
        )

    def t_copy(e, p):
        source, target, way = EDGES[e]
        first, amount = p * PIECE, PIECE
        return pltpu.make_async_remote_copy(
            src_ref=slots.at[source, pl.ds(first, amount), :],
            dst_ref=slots.at[target, pl.ds(first, amount), :],
            send_sem=t_send.at[e, p],
            recv_sem=t_recv.at[e, p],
            device_id=chip(0, 0, True) if way is None else chip(way[0], way[1], False),
            device_id_type=MESH,
        )

    def edges_of(p):
        return (0, 1, 2, 3, 4 + p % 2, 6, 7, 8)

    def go(p, *edges):
        for e in edges:
            if e in edges_of(p):
                t_copy(e, p).start()

    def come(p, *edges):
        for e in edges:
            if e in edges_of(p):
                t_copy(e, p).wait_recv()

    def root(p):
        if p:
            z_copy(p).wait_recv()
        go(p, 1, 0, 6)

    def into2(p):
        come(p, 1)
        go(p, 2, 3)

    def into1(p):
        come(p, 0)
        go(p, 7)

    def into3(p):
        come(p, 2)
        go(p, 4, 8)

    def into4(p):
        come(p, 3)
        go(p, 5)

    holder = group == z

    def a_copy(sender):
        return pltpu.make_async_remote_copy(
            src_ref=count.at[sender], dst_ref=count.at[sender], send_sem=a_send, recv_sem=a_recv.at[sender],
            device_id={"group": group, "tile": group * 4 + x}, device_id_type=MESH,
        )

    def b_copy(n):
        return pltpu.make_async_remote_copy(
            src_ref=total, dst_ref=spread.at[0], send_sem=b_send.at[n], recv_sem=b_recv,
            device_id={"group": (group + n) % 8, "tile": tile}, device_id_type=MESH,
        )

    def c_copy(n):
        return pltpu.make_async_remote_copy(
            src_ref=spread.at[0], dst_ref=spread.at[n], send_sem=c_send.at[n], recv_sem=c_recv.at[n],
            device_id={"group": group, "tile": z * 4 + (x + n) % 4}, device_id_type=MESH,
        )

    def bounds_a():
        @pl.when(jnp.logical_not(holder))
        def _():
            a_copy(z).start()

    def bounds_b():
        @pl.when(holder)
        def _():
            for n in range(1, 8):
                a_copy((z + n) % 8).wait_recv()
            value = count[0]
            for n in range(1, 8):
                value += count[n]
            total[...] = value
            spread[0] = value
            for n in range(1, 8):
                b_copy(n).start()

    def bounds_c():
        @pl.when(jnp.logical_not(holder))
        def _():
            b_copy(1).wait_recv()

        for n in range(1, 4):
            c_copy(n).start()

    def bounds_d():
        value = spread[0]
        for n in range(1, 4):
            c_copy(n).wait_recv()
            value += spread[n]
        bound[...] = jnp.broadcast_to(jnp.sum(value, axis=1, keepdims=True), (8, 128)).astype(jnp.int32)

    def bounds_end():
        @pl.when(jnp.logical_not(holder))
        def _():
            a_copy(z).wait_send()

        @pl.when(holder)
        def _():
            for n in range(1, 8):
                b_copy(n).wait_send()

        for n in range(1, 4):
            c_copy(n).wait_send()

    def identify(rows, cols):
        def offset_of(slot):
            nx, ny = place(*(COVER[slot] if slot < 6 else COVER[SIBLING[slot - 6]][::-1]))
            return nx * 512 + ny * 128 + (c if slot < 6 else 1 - c) * 64

        def steps_before(p):
            return ((z + OFFSETS[p] + 8) % 8) * 2048

        def cluster(position):
            ids = jnp.zeros(position.shape, jnp.int32)
            for m in range(1, 8):
                ids += jnp.where(position >= bound[m : m + 1, :], 1, 0)
            return ids

        for slot in rows:
            start = offset_of(slot)
            for p in range(8):
                position = (start + steps_before(p)) + lax.broadcasted_iota(jnp.int32, (PIECE, 128), 0)
                idr[slot, p * PIECE : (p + 1) * PIECE, :] = cluster(position)
        for slot in cols:
            start = offset_of(slot)
            for q in range(4):
                lane = lax.broadcasted_iota(jnp.int32, (8, 128), 1)
                position = jnp.where(lane < 64, start + steps_before(2 * q) + lane, start + steps_before(2 * q + 1) + lane - 64)
                idc[slot, :, q * 128 : (q + 1) * 128] = cluster(position)

    def clear():
        rowacc[...] = jnp.full(rowacc.shape, -1.0, jnp.float32)
        colacc[...] = jnp.full(colacc.shape, -1.0, jnp.float32)

    def score(i, j, rows, cols, diagonal=False):
        height = rows[1]
        rows = pl.ds(rows[0], height)
        scores = lax.dot_general(
            slots[i, rows, :], slots[j, pl.ds(cols[0], cols[1]), :], (((1,), (1,)), ((), ())),
            preferred_element_type=jnp.float32,
        )
        best = rowacc[i, rows, :]
        for m in range(cols[1] // 128):
            part = scores[:, m * 128 : (m + 1) * 128]
            at = cols[0] + m * 128
            at = pl.ds(at if isinstance(at, int) else pl.multiple_of(at, 128), 128)
            keep = idr[i, rows, :] == idc[j, 0:1, at]
            if diagonal:
                row = lax.broadcasted_iota(jnp.int32, (height, 128), 0)
                col = lax.broadcasted_iota(jnp.int32, (height, 128), 1) + m * 128
                keep = jnp.logical_and(keep, row != col)
            part = jnp.where(keep, part, -1.0)
            best = jnp.maximum(best, part)
            colacc[j, :, at] = jnp.maximum(colacc[j, :, at], jnp.max(part.reshape(height // 8, 8, 128), axis=0))
        rowacc[i, rows, :] = best

    def loop(table, body, together):
        def step(n, carry):
            for at in range(together):
                body([pick(n, column) for column in zip(*table[at::together])])
            return carry

        if len(table) == together:
            for entry in table:
                body(entry)
        else:
            lax.fori_loop(0, len(table) // together, step, 0)

    def early(entry):
        score(entry[0], entry[1], (0, 256), (0, 256))

    def late(entry):
        score(entry[0], entry[1], (0, 512), (256, 256))
        score(entry[0], entry[1], (256, 256), (0, 256))

    def half(entry):
        i, j, kind = entry
        h = jnp.where(kind == 0, v // 2, jnp.where(kind == 1, u // 2, c))
        h = pl.multiple_of(h * 256, 256)
        score(i, j, (0, 256), (256, 256))
        score(i, j, (h, 256), (h, 256))

    def settle(slot):
        res[slot] = jnp.max(rowacc[slot].T, axis=0, keepdims=True)

    def finish(slot):
        best = jnp.max(colacc[slot], axis=0, keepdims=True)
        res[slot] = jnp.maximum(best, res[slot]) if slot < 6 else best

    def r_copy(slot):
        du, dv = COVER[slot] if slot < 6 else COVER[SIBLING[slot - 6]][::-1]
        return pltpu.make_async_remote_copy(
            src_ref=res.at[slot], dst_ref=inb.at[slot], send_sem=r_send.at[slot], recv_sem=r_recv.at[slot],
            device_id=chip(du, dv, slot >= 6), device_id_type=MESH,
        )

    def answer(*chosen):
        for slot in chosen:
            finish(slot)
            r_copy(slot).start()

    bounds_a()
    for p in range(1, 3):
        z_copy(p).start()
    root(0)
    for p in range(3, 8):
        z_copy(p).start()
    clear()
    root(1)
    root(2)
    bounds_b()
    into2(0)
    into1(0)
    root(3)
    into2(1)
    into1(1)
    root(4)
    into2(2)
    into1(2)
    into3(0)
    into4(0)
    root(5)
    into2(3)
    into1(3)
    bounds_c()
    into3(1)
    into4(1)
    root(6)
    into2(4)
    into1(4)
    into3(2)
    into4(2)
    root(7)
    into2(5)
    into4(3)
    into3(3)
    bounds_d()
    identify((0, 1, 2), ())
    into2(6)
    into1(5)
    into3(4)
    into4(4)
    identify((3, 4, 5), ())
    identify((), (0, 1, 2, 3, 4, 6, 7, 8))
    into2(7)
    into4(5)
    loop(FULL[:4], early, 4)
    into1(7)
    loop(FULL[:1], late, 1)
    into1(6)
    into3(6)
    into3(5)
    for p in range(4):
        come(p, 4, 5)
    loop(FULL[8:9], early, 1)
    score(0, 0, (0, 256), (0, 256), True)
    into4(6)
    for p in range(4):
        come(p, 6, 8)
    loop(FULL[4:8], early, 4)
    loop(FULL[9:], early, 2)
    for p in range(4, 8):
        come(p, 6)
    loop(FULL[4:6], late, 2)
    loop(HALF[2:3], half, 1)
    into4(7)
    loop(FULL[3:4], late, 1)
    loop(FULL[6:7], late, 1)
    loop(HALF[:2], half, 2)
    score(0, 0, (0, 256), (256, 256))
    score(0, 0, (256, 256), (256, 256), True)
    into3(7)
    loop(FULL[1:3], late, 2)
    loop(HALF[3:5], half, 2)
    for p in range(4, 8):
        come(p, 8)
    loop(FULL[7:8], late, 1)
    for p in range(8):
        come(p, 7)
    loop(HALF[5:7], half, 2)
    for slot in (3, 4, 0, 1, 2):
        settle(slot)
    answer(3, 4, 7)
    for p in range(4, 8):
        come(p, 4, 5)
    loop(FULL[8:], late, 3)
    loop(HALF[7:], half, 2)
    settle(5)
    answer(5, 8, 1, 2, 6)
    finish(0)
    bounds_end()
    for p in range(8):
        if p:
            z_copy(p).wait_send()
        for e in edges_of(p):
            t_copy(e, p).wait_send()

    best = res[0]
    for slot in (3, 4, 7, 5, 1, 2, 6, 8):
        r_copy(slot).wait_recv()
        best = jnp.maximum(best, inb[slot])
    lane = lax.broadcasted_iota(jnp.int32, (1, 128), 1)
    for p in range(8):
        part = best[:, p // 2 * 128 : (p // 2 + 1) * 128]
        turned = pltpu.roll(part, 64, 1)
        near[p] = jnp.where((lane < 64) == (p % 2 == 0), part, turned)

    def o_copy(p):
        return pltpu.make_async_remote_copy(
            src_ref=near.at[p], dst_ref=obuf.at[z], send_sem=o_send.at[p], recv_sem=o_recv.at[p],
            device_id=plane(OFFSETS[p]), device_id_type=MESH,
        )

    for p in (7, 5, 6, 3, 4, 1, 2):
        o_copy(p).start()
    obuf[z] = near[0]
    for slot in range(1, 9):
        r_copy(slot).wait_send()
    for p in (1, 2, 3, 4, 5, 6, 7):
        o_copy(p).wait_recv()
    for q in range(4):
        out_ref[:, q * 128 : (q + 1) * 128] = jnp.where(lane < 64, obuf[2 * q], obuf[2 * q + 1])
    for p in range(1, 8):
        o_copy(p).wait_send()


def local(embeddings, cluster_ids):
    dma = pltpu.SemaphoreType.DMA
    return pl.pallas_call(
        kernel,
        out_shape=jax.ShapeDtypeStruct((1, ROWS), jnp.float32),
        in_specs=[pl.BlockSpec(memory_space=pl.ANY), pl.BlockSpec(memory_space=pltpu.VMEM)],
        out_specs=pl.BlockSpec(memory_space=pltpu.VMEM),
        scratch_shapes=[
            pltpu.VMEM((8, PIECE, D), jnp.bfloat16),
            pltpu.VMEM((8, PIECE, D), jnp.bfloat16),
            pltpu.VMEM((9, ROWS, D), jnp.bfloat16),
            pltpu.VMEM((6, ROWS, 128), jnp.int32),
            pltpu.VMEM((9, 8, ROWS), jnp.int32),
            pltpu.VMEM((6, ROWS, 128), jnp.float32),
            pltpu.VMEM((9, 8, ROWS), jnp.float32),
            pltpu.VMEM((9, 1, ROWS), jnp.float32),
            pltpu.VMEM((9, 1, ROWS), jnp.float32),
            pltpu.VMEM((8, 1, 128), jnp.float32),
            pltpu.VMEM((8, 1, 128), jnp.float32),
            pltpu.VMEM((8, 8, 128), jnp.float32),
            pltpu.VMEM((8, 128), jnp.float32),
            pltpu.VMEM((4, 8, 128), jnp.float32),
            pltpu.VMEM((8, 128), jnp.int32),
            dma((8,)), dma((8,)), dma((8,)), dma((9, 8)), dma((9, 8)), dma((9,)), dma((9,)), dma((8,)), dma((8,)),
            dma, dma((8,)), dma((8,)), dma, dma((4,)), dma((4,)),
        ],
        compiler_params=pltpu.CompilerParams(
            collective_id=0, has_side_effects=True, vmem_limit_bytes=40 * 1024 * 1024
        ),
        cost_estimate=pl.CostEstimate(flops=2 * 17 * 512 * 512 * 768, bytes_accessed=1 << 20, transcendentals=0),
    )(embeddings, cluster_ids)


def solution(mesh):
    in_specs = (P("group", "tile", None), P("group", "tile"))
    out_specs = P("group", "tile")
    return jax.shard_map(local, mesh=mesh, in_specs=in_specs, out_specs=out_specs, check_vma=False)
```

```python
import functools

import jax
import jax.numpy as jnp
from jax import lax
from jax.experimental import pallas as pl
from jax.experimental.pallas import tpu as pltpu
from jax.sharding import PartitionSpec as P

MESH = pl.DeviceIdType.MESH
D = 768
ROWS = 512
PIECE = 64

COVER = ((0, 0), (0, 1), (0, -1), (1, -1), (-1, -1), (2, -1))
SIBLING = (0, 1, 3)
OFFSETS = (0, 1, -1, 2, -2, 3, -3, 4)
FULL = ((0, 2), (0, 3), (2, 3), (0, 4), (2, 6), (1, 6), (4, 6), (4, 8), (5, 0), (5, 6), (5, 8))
HALF = ((1, 2, 0), (1, 4, 0), (0, 6, 2), (1, 3, 0), (3, 6, 2), (3, 8, 2), (1, 7, 2), (5, 1, 0), (5, 2, 1))
EDGES = (
    (0, 1, (0, -1)), (0, 2, (0, 1)), (2, 3, (-1, 0)), (2, 4, (1, 0)), (3, 5, (-1, 0)), (4, 5, (1, 0)),
    (0, 6, None), (1, 7, None), (3, 8, None),
)


def pick(n, table):
    value = jnp.int32(table[0])
    for at in range(1, len(table)):
        value = jnp.where(n == at, jnp.int32(table[at]), value)
    return value


def kernel(
    x_ref, id_ref, out_ref,
    raw, unit, slots, idr, idc, rowacc, colacc, res, inb, near, obuf, count, total, spread, bound,
    x_sem, z_send, z_recv, t_send, t_recv, r_send, r_recv, o_send, o_recv,
    a_send, a_recv, b_send, b_recv, c_send, c_recv,
):
    group = lax.axis_index("group")
    tile = lax.axis_index("tile")
    y, c = group // 2, group % 2
    z, x = tile // 4, tile % 4
    flip = c == 1
    u = jnp.where(flip, y, x)
    v = jnp.where(flip, x, y)

    def place(du, dv):
        nu, nv = (u + du + 4) % 4, (v + dv + 4) % 4
        return jnp.where(flip, nv, nu), jnp.where(flip, nu, nv)

    def chip(du, dv, other, dz=0):
        nx, ny = place(du, dv)
        nc = 1 - c if other else c
        return {"group": ny * 2 + nc, "tile": ((z + dz + 8) % 8) * 4 + nx}

    def plane(dz):
        return {"group": group, "tile": ((z + dz + 8) % 8) * 4 + x}

    def input_copy(p):
        k = (z - OFFSETS[p] + 8) % 8
        rows = pl.ds(pl.multiple_of(k * PIECE, PIECE), PIECE)
        return pltpu.make_async_copy(x_ref.at[0, rows, :], raw.at[p], x_sem.at[p])

    for p in range(8):
        input_copy(p).start()

    barrier = pltpu.get_barrier_semaphore()
    partners = [plane(o) for o in range(1, 8)]
    partners += [chip(a, b, False) for a, b in ((0, 1), (0, -1), (1, 0), (-1, 0), (1, -1), (-1, 1), (-1, -1), (1, 1), (2, -1), (2, 1), (0, 2), (2, 0))]
    partners += [chip(a, b, True) for a, b in ((0, 0), (1, 0), (0, -1), (-1, 1))]
    partners += [chip(jnp.where(flip, -1, 0), jnp.where(flip, 0, 1), True), chip(jnp.where(flip, 2, 0), jnp.where(flip, 0, 2), True)]
    for partner in partners:
        pl.semaphore_signal(barrier, inc=1, device_id=partner, device_id_type=MESH)

    def normalize(p):
        input_copy(p).wait()
        values = raw[p].astype(jnp.float32)
        size = jnp.sum(values * values, axis=1, keepdims=True) + 1e-06
        return (values * (1.0 / jnp.sqrt(size))).astype(jnp.bfloat16)

    slots[0, 0:PIECE, :] = normalize(0)
    for p in range(1, 8):
        unit[p] = normalize(p)
    for m in range(8):
        below = jnp.zeros((1, 128), jnp.float32)
        for q in range(4):
            below += jnp.where(id_ref[:, q * 128 : (q + 1) * 128] < m, 1.0, 0.0)
        count[z, m : m + 1, :] = below

    pl.semaphore_wait(barrier, len(partners))

    def z_copy(p):
        return pltpu.make_async_remote_copy(
            src_ref=unit.at[p],
            dst_ref=slots.at[0, pl.ds(p * PIECE, PIECE), :],
            send_sem=z_send.at[p],
            recv_sem=z_recv.at[p],
            device_id=plane(-OFFSETS[p]),
            device_id_type=MESH,
        )

    def t_copy(e, p):
        source, target, way = EDGES[e]
        first, amount = p * PIECE, PIECE
        return pltpu.make_async_remote_copy(
            src_ref=slots.at[source, pl.ds(first, amount), :],
            dst_ref=slots.at[target, pl.ds(first, amount), :],
            send_sem=t_send.at[e, p],
            recv_sem=t_recv.at[e, p],
            device_id=chip(0, 0, True) if way is None else chip(way[0], way[1], False),
            device_id_type=MESH,
        )

    def edges_of(p):
        return (0, 1, 2, 3, 4 + p % 2, 6, 7, 8)

    def go(p, *edges):
        for e in edges:
            if e in edges_of(p):
                t_copy(e, p).start()

    def come(p, *edges):
        for e in edges:
            if e in edges_of(p):
                t_copy(e, p).wait_recv()

    def root(p):
        if p:
            z_copy(p).wait_recv()
        go(p, 1, 0, 6)

    def into2(p):
        come(p, 1)
        go(p, 2, 3)

    def into1(p):
        come(p, 0)
        go(p, 7)

    def into3(p):
        come(p, 2)
        go(p, 4, 8)

    def into4(p):
        come(p, 3)
        go(p, 5)

    holder = group == z

    def a_copy(sender):
        return pltpu.make_async_remote_copy(
            src_ref=count.at[sender], dst_ref=count.at[sender], send_sem=a_send, recv_sem=a_recv.at[sender],
            device_id={"group": group, "tile": group * 4 + x}, device_id_type=MESH,
        )

    def b_copy(n):
        return pltpu.make_async_remote_copy(
            src_ref=total, dst_ref=spread.at[0], send_sem=b_send.at[n], recv_sem=b_recv,
            device_id={"group": (group + n) % 8, "tile": tile}, device_id_type=MESH,
        )

    def c_copy(n):
        return pltpu.make_async_remote_copy(
            src_ref=spread.at[0], dst_ref=spread.at[n], send_sem=c_send.at[n], recv_sem=c_recv.at[n],
            device_id={"group": group, "tile": z * 4 + (x + n) % 4}, device_id_type=MESH,
        )

    def bounds_a():
        @pl.when(jnp.logical_not(holder))
        def _():
            a_copy(z).start()

    def bounds_b():
        @pl.when(holder)
        def _():
            for n in range(1, 8):
                a_copy((z + n) % 8).wait_recv()
            value = count[0]
            for n in range(1, 8):
                value += count[n]
            total[...] = value
            spread[0] = value
            for n in range(1, 8):
                b_copy(n).start()

    def bounds_c():
        @pl.when(jnp.logical_not(holder))
        def _():
            b_copy(1).wait_recv()

        for n in range(1, 4):
            c_copy(n).start()

    def bounds_d():
        value = spread[0]
        for n in range(1, 4):
            c_copy(n).wait_recv()
            value += spread[n]
        bound[...] = jnp.broadcast_to(jnp.sum(value, axis=1, keepdims=True), (8, 128)).astype(jnp.int32)

    def bounds_end():
        @pl.when(jnp.logical_not(holder))
        def _():
            a_copy(z).wait_send()

        @pl.when(holder)
        def _():
            for n in range(1, 8):
                b_copy(n).wait_send()

        for n in range(1, 4):
            c_copy(n).wait_send()

    def identify(rows, cols):
        def offset_of(slot):
            nx, ny = place(*(COVER[slot] if slot < 6 else COVER[SIBLING[slot - 6]][::-1]))
            return nx * 512 + ny * 128 + (c if slot < 6 else 1 - c) * 64

        def steps_before(p):
            return ((z + OFFSETS[p] + 8) % 8) * 2048

        def cluster(position):
            ids = jnp.zeros(position.shape, jnp.int32)
            for m in range(1, 8):
                ids += jnp.where(position >= bound[m : m + 1, :], 1, 0)
            return ids

        for slot in rows:
            start = offset_of(slot)
            for p in range(8):
                position = (start + steps_before(p)) + lax.broadcasted_iota(jnp.int32, (PIECE, 128), 0)
                idr[slot, p * PIECE : (p + 1) * PIECE, :] = cluster(position)
        for slot in cols:
            start = offset_of(slot)
            for q in range(4):
                lane = lax.broadcasted_iota(jnp.int32, (8, 128), 1)
                position = jnp.where(lane < 64, start + steps_before(2 * q) + lane, start + steps_before(2 * q + 1) + lane - 64)
                idc[slot, :, q * 128 : (q + 1) * 128] = cluster(position)

    def clear():
        rowacc[...] = jnp.full(rowacc.shape, -1.0, jnp.float32)
        colacc[...] = jnp.full(colacc.shape, -1.0, jnp.float32)

    def score(i, j, rows, cols, diagonal=False):
        height = rows[1]
        rows = pl.ds(rows[0], height)
        scores = lax.dot_general(
            slots[i, rows, :], slots[j, pl.ds(cols[0], cols[1]), :], (((1,), (1,)), ((), ())),
            preferred_element_type=jnp.float32,
        )
        best = rowacc[i, rows, :]
        for m in range(cols[1] // 128):
            part = scores[:, m * 128 : (m + 1) * 128]
            at = cols[0] + m * 128
            at = pl.ds(at if isinstance(at, int) else pl.multiple_of(at, 128), 128)
            keep = idr[i, rows, :] == idc[j, 0:1, at]
            if diagonal:
                row = lax.broadcasted_iota(jnp.int32, (height, 128), 0)
                col = lax.broadcasted_iota(jnp.int32, (height, 128), 1) + m * 128
                keep = jnp.logical_and(keep, row != col)
            part = jnp.where(keep, part, -1.0)
            best = jnp.maximum(best, part)
            colacc[j, :, at] = jnp.maximum(colacc[j, :, at], jnp.max(part.reshape(height // 8, 8, 128), axis=0))
        rowacc[i, rows, :] = best

    def loop(table, body, together):
        def step(n, carry):
            for at in range(together):
                body([pick(n, column) for column in zip(*table[at::together])])
            return carry

        if len(table) == together:
            for entry in table:
                body(entry)
        else:
            lax.fori_loop(0, len(table) // together, step, 0)

    def early(entry):
        score(entry[0], entry[1], (0, 256), (0, 256))

    def late(entry):
        score(entry[0], entry[1], (0, 512), (256, 256))
        score(entry[0], entry[1], (256, 256), (0, 256))

    def half(entry):
        i, j, kind = entry
        h = jnp.where(kind == 0, v // 2, jnp.where(kind == 1, u // 2, c))
        h = pl.multiple_of(h * 256, 256)
        score(i, j, (0, 256), (256, 256))
        score(i, j, (h, 256), (h, 256))

    def settle(slot):
        res[slot] = jnp.max(rowacc[slot].T, axis=0, keepdims=True)

    def finish(slot):
        best = jnp.max(colacc[slot], axis=0, keepdims=True)
        res[slot] = jnp.maximum(best, res[slot]) if slot < 6 else best

    def r_copy(slot):
        du, dv = COVER[slot] if slot < 6 else COVER[SIBLING[slot - 6]][::-1]
        return pltpu.make_async_remote_copy(
            src_ref=res.at[slot], dst_ref=inb.at[slot], send_sem=r_send.at[slot], recv_sem=r_recv.at[slot],
            device_id=chip(du, dv, slot >= 6), device_id_type=MESH,
        )

    def answer(*chosen):
        for slot in chosen:
            finish(slot)
            r_copy(slot).start()

    bounds_a()
    for p in range(1, 3):
        z_copy(p).start()
    root(0)
    for p in range(3, 8):
        z_copy(p).start()
    clear()
    root(1)
    root(2)
    bounds_b()
    into2(0)
    into1(0)
    root(3)
    into2(1)
    into1(1)
    root(4)
    into2(2)
    into1(2)
    into3(0)
    into4(0)
    root(5)
    into2(3)
    into1(3)
    bounds_c()
    into3(1)
    into4(1)
    root(6)
    into2(4)
    into1(4)
    into3(2)
    into4(2)
    root(7)
    into2(5)
    into4(3)
    into3(3)
    into2(6)
    into1(5)
    into3(4)
    into4(4)
    bounds_d()
    identify((0, 1, 2), ())
    into2(7)
    into4(5)
    identify((3, 4, 5), ())
    identify((), (0, 1, 2, 3, 4, 6, 7, 8))
    loop(FULL[:4], early, 4)
    into1(7)
    loop(FULL[:1], late, 1)
    into1(6)
    into3(6)
    into3(5)
    for p in range(4):
        come(p, 4, 5)
    loop(FULL[8:9], early, 1)
    score(0, 0, (0, 256), (0, 256), True)
    into4(6)
    for p in range(4):
        come(p, 6, 8)
    loop(FULL[4:8], early, 4)
    loop(FULL[9:], early, 2)
    for p in range(4, 8):
        come(p, 6)
    loop(FULL[4:6], late, 2)
    loop(HALF[2:3], half, 1)
    into4(7)
    loop(FULL[3:4], late, 1)
    loop(FULL[6:7], late, 1)
    loop(HALF[:2], half, 2)
    score(0, 0, (0, 256), (256, 256))
    score(0, 0, (256, 256), (256, 256), True)
    into3(7)
    loop(FULL[1:3], late, 2)
    loop(HALF[3:5], half, 2)
    for p in range(4, 8):
        come(p, 8)
    loop(FULL[7:8], late, 1)
    for p in range(8):
        come(p, 7)
    loop(HALF[5:7], half, 2)
    for slot in (3, 4, 0, 1, 2):
        settle(slot)
    answer(3, 4, 7)
    for p in range(4, 8):
        come(p, 4, 5)
    loop(FULL[8:], late, 3)
    loop(HALF[7:], half, 2)
    settle(5)
    answer(5, 8, 1, 2, 6)
    finish(0)
    bounds_end()
    for p in range(8):
        if p:
            z_copy(p).wait_send()
        for e in edges_of(p):
            t_copy(e, p).wait_send()

    best = res[0]
    for slot in (3, 4, 7, 5, 1, 2, 6, 8):
        r_copy(slot).wait_recv()
        best = jnp.maximum(best, inb[slot])
    lane = lax.broadcasted_iota(jnp.int32, (1, 128), 1)
    for p in range(8):
        part = best[:, p // 2 * 128 : (p // 2 + 1) * 128]
        turned = pltpu.roll(part, 64, 1)
        near[p] = jnp.where((lane < 64) == (p % 2 == 0), part, turned)

    def o_copy(p):
        return pltpu.make_async_remote_copy(
            src_ref=near.at[p], dst_ref=obuf.at[z], send_sem=o_send.at[p], recv_sem=o_recv.at[p],
            device_id=plane(OFFSETS[p]), device_id_type=MESH,
        )

    for p in (7, 5, 6, 3, 4, 1, 2):
        o_copy(p).start()
    obuf[z] = near[0]
    for slot in range(1, 9):
        r_copy(slot).wait_send()
    for p in (1, 2, 3, 4, 5, 6, 7):
        o_copy(p).wait_recv()
    for q in range(4):
        out_ref[:, q * 128 : (q + 1) * 128] = jnp.where(lane < 64, obuf[2 * q], obuf[2 * q + 1])
    for p in range(1, 8):
        o_copy(p).wait_send()


def local(embeddings, cluster_ids):
    dma = pltpu.SemaphoreType.DMA
    return pl.pallas_call(
        kernel,
        out_shape=jax.ShapeDtypeStruct((1, ROWS), jnp.float32),
        in_specs=[pl.BlockSpec(memory_space=pl.ANY), pl.BlockSpec(memory_space=pltpu.VMEM)],
        out_specs=pl.BlockSpec(memory_space=pltpu.VMEM),
        scratch_shapes=[
            pltpu.VMEM((8, PIECE, D), jnp.bfloat16),
            pltpu.VMEM((8, PIECE, D), jnp.bfloat16),
            pltpu.VMEM((9, ROWS, D), jnp.bfloat16),
            pltpu.VMEM((6, ROWS, 128), jnp.int32),
            pltpu.VMEM((9, 8, ROWS), jnp.int32),
            pltpu.VMEM((6, ROWS, 128), jnp.float32),
            pltpu.VMEM((9, 8, ROWS), jnp.float32),
            pltpu.VMEM((9, 1, ROWS), jnp.float32),
            pltpu.VMEM((9, 1, ROWS), jnp.float32),
            pltpu.VMEM((8, 1, 128), jnp.float32),
            pltpu.VMEM((8, 1, 128), jnp.float32),
            pltpu.VMEM((8, 8, 128), jnp.float32),
            pltpu.VMEM((8, 128), jnp.float32),
            pltpu.VMEM((4, 8, 128), jnp.float32),
            pltpu.VMEM((8, 128), jnp.int32),
            dma((8,)), dma((8,)), dma((8,)), dma((9, 8)), dma((9, 8)), dma((9,)), dma((9,)), dma((8,)), dma((8,)),
            dma, dma((8,)), dma((8,)), dma, dma((4,)), dma((4,)),
        ],
        compiler_params=pltpu.CompilerParams(
            collective_id=0, has_side_effects=True, vmem_limit_bytes=40 * 1024 * 1024
        ),
        cost_estimate=pl.CostEstimate(flops=2 * 17 * 512 * 512 * 768, bytes_accessed=1 << 20, transcendentals=0),
    )(embeddings, cluster_ids)


def solution(mesh):
    in_specs = (P("group", "tile", None), P("group", "tile"))
    out_specs = P("group", "tile")
    return jax.shard_map(local, mesh=mesh, in_specs=in_specs, out_specs=out_specs, check_vma=False)
```
